32 devices in a mesh: pool: 4 (over y, core), tgt: 8 (over z, x).
Axes of the slice: x: 2, y: 2, z: 4, core: 2. Of those that a mesh axis runs over, the one named last changes fastest.
Arguments:
- pool_grads: bfloat16 [8192, 16384], P('pool', 'tgt'), may hold values from -6 to 6
- target_grads: bfloat16 [512, 16384], P('pool', 'tgt'), may hold values from -6 to 6
- precond: bfloat16 [32, 512, 512], P('tgt'), as said below
- active: int32 [4, 16], replicated, may hold values from 0 to 31, as said below
Outputs:
- scores: float32 [8192, 512], P(('pool', 'tgt'))
The draws below stay inside these ranges and needn't reach their ends.
Inputs may be any that keep to these rules, and one draw needn't show every extreme that they name: `active`: each row lists 16 distinct blocks; rows 2k and 2k + 1 together list every block exactly once. `precond`: each block is symmetric with a positive diagonal.
All inputs are finite; a program needn't handle non-finite values.
Results may differ from the reference program's by a relative error of at most 0.0029.
Values may be sent and summed in bfloat16 or wider, within the bound.
No kernel may reach another device: no remote copies, remote signals or barrier semaphores. Data moves between devices by JAX's collectives and lax.ppermute only.
A program may use at most 64 MiB of HBM per device.

```python
import math
import jax
import jax.numpy as jnp
from jax import lax

BS = 512
BLK_DEV = 4
PANELS = 4
PROWS = 128
NB = 32
G = 16384
NACT = 16
TROWS = 512
POOL = 8192


def draw_precond(key, part):
    first, second = jax.random.split(key)
    noise = jax.random.normal(first, (NB, BS, BS), jnp.float32)
    noise = (noise + jnp.swapaxes(noise, 1, 2)) * (0.5 / math.sqrt(2.0 * BS))
    diag = jnp.exp(jax.random.uniform(second, (NB, BS), jnp.float32, math.log(0.5), math.log(2.0)))
    ident = jnp.eye(BS, dtype=jnp.float32)
    return (noise * (1.0 - ident) + diag[:, :, None] * ident).astype(jnp.bfloat16)


def draw_active(key, part):
    keys = jax.random.split(key, PANELS // 2)
    orders = jax.vmap(lambda one: jax.random.permutation(one, NB))(keys)
    return orders.reshape(PANELS, NACT).astype(jnp.int32)


def strengthened(result, own_key, source, target, shards_of, factor):
    owner, partner = [(jnp.arange(result.shape[position]) // (result.shape[position] // shards_of)).reshape([-1 if axis == position else 1 for axis in range(result.ndim)]) for position in (source, target)]
    chosen = jax.random.permutation(own_key, shards_of)[partner]
    strong = (owner == chosen) | (owner == (partner + shards_of // 2) % shards_of)
    return jnp.where(strong, factor * result, result)


def level_of(rng, shape, cuts, least, high):
    level, own = 1.0, jax.random.fold_in(rng, 6)
    for axis_at, shards_of in cuts:
        draws = jnp.exp(jax.random.uniform(jax.random.fold_in(own, axis_at), (shards_of,), jnp.float32, least / len(cuts), high / len(cuts)))
        level = level * jnp.repeat(draws, shape[axis_at] // shards_of).reshape([-1 if axis == axis_at else 1 for axis in range(len(shape))])
    return level


def bell_draw(own_key, dims, spread, limit, shards=(), kind=jnp.bfloat16):
    result = spread * jax.random.normal(own_key, dims, jnp.float32)
    if shards:
        result = result * level_of(own_key, dims, shards, -0.22, 0.18)
    return jnp.clip(result, -limit, limit).astype(kind)


def gaussian_with(rng, dims, spread, bound, pieces, heavy, held_as=jnp.bfloat16):
    result = spread * jax.random.normal(rng, dims, jnp.float32)
    if pieces:
        result = result * level_of(rng, dims, pieces, -0.22, 0.18)
    return jnp.clip(strengthened(result, jax.random.fold_in(rng, 3), *heavy), -bound, bound).astype(held_as)


def setup_inputs(seed: int = 0) -> dict:
    arg_keys = jax.random.split(jax.random.key(seed), 5)
    pool_grads = gaussian_with(arg_keys[0], (POOL, G), 1.0, 6.0, ((0, 4), (1, 8)), (1, 0, 8, 2.0))
    target_grads = bell_draw(arg_keys[1], (TROWS, G), 1.0, 6.0, ((0, 4), (1, 8)))
    precond = draw_precond(jax.random.fold_in(arg_keys[4], 71), 0)
    active = draw_active(jax.random.fold_in(arg_keys[4], 71), 0)
    return dict(pool_grads=pool_grads, target_grads=target_grads, precond=precond, active=active)


def reference(pool_grads, target_grads, precond, active):
    nblocks = precond.shape[0]
    bsize = precond.shape[1]
    hits = (active[:, :, None] == jnp.arange(nblocks, dtype=jnp.int32)[None, None, :]).astype(jnp.float32)
    mask = jnp.sum(hits, axis=1)
    row_mask = jnp.repeat(mask, PROWS, axis=0)
    scale = (NACT * BS) ** -0.5
    rows = target_grads.astype(jnp.float32).reshape(TROWS, nblocks, bsize)
    conditioned = jnp.einsum("rbi,bij->rbj", rows, precond.astype(jnp.float32))
    conditioned = (conditioned * row_mask[:, :, None] * scale).astype(jnp.bfloat16).reshape(TROWS, nblocks * bsize)
    width = BLK_DEV * BS
    groups = nblocks // BLK_DEV

    def add_group(total, index):
        start = (index * width).astype(jnp.int32)
        left = lax.dynamic_slice_in_dim(pool_grads, start, width, 1)
        right = lax.dynamic_slice_in_dim(conditioned, start, width, 1)
        partial_value = lax.dot_general(left, right, (((1,), (1,)), ((), ())), preferred_element_type=jnp.float32)
        return total + partial_value, None

    start_total = jnp.zeros((pool_grads.shape[0], TROWS), jnp.float32)
    scores, _ = lax.scan(add_group, start_total, jnp.arange(groups, dtype=jnp.int32))
    return scores
```

```python
import functools

import jax
import jax.numpy as jnp
from jax import lax
from jax.experimental import pallas as pl
from jax.experimental.pallas import tpu as pltpu
from jax.sharding import PartitionSpec as P

PROWS = 128
F32, BF16 = jnp.float32, jnp.bfloat16
VMEM = pl.BlockSpec(memory_space=pltpu.VMEM)


def call(body, outs, *args, flops=0, mib=20, scratch=()):
    return pl.pallas_call(
        body,
        in_specs=[VMEM] * len(args),
        out_specs=[VMEM] * len(outs),
        out_shape=[jax.ShapeDtypeStruct(shape, dtype) for shape, dtype in outs],
        scratch_shapes=list(scratch),
        compiler_params=pltpu.CompilerParams(vmem_limit_bytes=mib * 2**20),
        cost_estimate=pl.CostEstimate(flops=flops, bytes_accessed=0, transcendentals=0),
    )(*args)


def listed(active, panel, block):
    rows = lax.broadcasted_iota(jnp.int32, active.shape, 0)
    return jnp.max(((active == block) & (rows == panel)).astype(jnp.int32))


def place(group):
    return lax.axis_index("tgt"), lax.axis_index("pool") // group


def near_kernel(group, scale, active, own, sib, pre, right, half):
    j, panel = place(group)
    core = panel & 1
    blocks, bs, _ = pre.shape
    depth = blocks // 2
    table = active[...]
    for b in range(blocks):
        even = listed(table, panel - core, j * blocks + b) == 1
        columns = slice(b * bs, (b + 1) * bs)
        mine = even == (core == 0)
        rows = jnp.where(mine, own[:, columns], sib[:, columns])
        product = jnp.dot(rows, pre[b], preferred_element_type=F32)
        value = (product * scale).T.astype(BF16)
        spread(right, value, even, b, bs)

        @pl.when(core == b // depth)
        def _():
            half[(b % depth) * bs : (b % depth + 1) * bs, :] = value


def spread(right, value, even, b, bs):
    zero = jnp.zeros_like(value)
    right[b * bs : (b + 1) * bs, :PROWS] = jnp.where(even, value, zero)
    right[b * bs : (b + 1) * bs, PROWS:] = jnp.where(even, zero, value)


def scores(pool, right, parts, j, send_a, keep_a, send_c, keep_c):
    rows = pool.shape[0] // parts
    low, high = j & 1, (j >> 1) & 1
    for da in (1, 0):
        for dc in (1, 0):
            for i in range(parts // 4):
                at = (i << 2) | ((high ^ dc) << 1) | (low ^ da)
                start = pl.multiple_of(at * rows, rows)
                value = jnp.dot(pool[pl.ds(start, rows), :], right[...], preferred_element_type=F32)
                out_a, out_c = (send_a if da else keep_a), (send_c if dc else keep_c)
                out_a[(i << 1) | (high ^ dc)] = value[:, :PROWS].astype(out_a.dtype)
                out_c[(i << 1) | (low ^ da)] = value[:, PROWS:].astype(out_c.dtype)


def scores_near_kernel(parts, pool, right, *outs):
    scores(pool, right, parts, lax.axis_index("tgt"), *outs)


def scores_far_kernel(parts, group, blocks, bs, active, pool, mine, other, *rest):
    outs, right = rest[:-1], rest[-1]
    j, panel = place(group)
    core = panel & 1
    depth = blocks // 2
    far = (panel ^ 2) - core
    table = active[...]
    for b in range(blocks):
        here = slice((b % depth) * bs, (b % depth + 1) * bs)
        value = jnp.where(core == b // depth, mine[here, :], other[here, :])
        spread(right, value, listed(table, far, j * blocks + b) == 1, b, bs)
    scores(pool, right, parts, j, *outs)


def halve_kernel(bit, count, *refs):
    keeps, gots, (send, keep) = refs[:count], refs[count : 2 * count], refs[2 * count :]
    value = (lax.axis_index("tgt") >> bit) & 1
    for i in range(send.shape[0]):
        for c in range(count):
            width = keeps[c].shape[2]
            columns = slice(c * width, (c + 1) * width)
            away, home = 2 * i + 1 - value, 2 * i + value
            send[i, :, columns] = (keeps[c][away] + gots[c][away].astype(F32)).astype(BF16)
            keep[i, :, columns] = keeps[c][home] + gots[c][home].astype(F32)


def halve(keeps, gots, bit):
    n, rows, width = keeps[0].shape
    shape = (n // 2, rows, width * len(keeps))
    return call(
        functools.partial(halve_kernel, bit, len(keeps)), [(shape, BF16), (shape, F32)], *keeps, *gots
    )


def last_kernel(group, near, near_got, far, far_got, out):
    _, panel = place(group)
    pair = panel >> 1
    width = near.shape[2]
    first, second = near[0] + near_got[0].astype(F32), far[0] + far_got[0].astype(F32)
    swapped = pair == 1
    out[:, :width] = jnp.where(swapped, second, first)
    out[:, width:] = jnp.where(swapped, first, second)


def local(tgt_size, pool_size, pool, target, pre, active):
    blocks, bs, _ = pre.shape
    scale = (active.shape[1] * bs) ** (-0.5)
    group = PROWS // target.shape[0]
    m, k = pool.shape
    part = m // tgt_size
    pool = pltpu.with_memory_space_constraint(pool, pltpu.VMEM)
    if group == 1:
        own = target
    else:
        groups = [list(range(g, g + group)) for g in range(0, pool_size, group)]
        own = lax.all_gather(target, "pool", axis=0, tiled=True, axis_index_groups=groups)

    def swap(x, axis, step):
        size = {"tgt": tgt_size, "pool": pool_size}[axis]
        return lax.ppermute(x, axis, [(i, i ^ step) for i in range(size)])

    sibling = swap(own, "pool", group)
    right, half = call(
        functools.partial(near_kernel, group, scale),
        [((k, 2 * PROWS), BF16), ((k // 2, PROWS), BF16)],
        active, own, sibling, pre, flops=2 * PROWS * k * bs,
    )
    mine = swap(half, "pool", 2 * group)
    other = swap(mine, "pool", group)
    shape = (tgt_size // 2, part, PROWS)
    outs = [(shape, BF16), (shape, F32)] * 2
    flops = 4 * m * k * PROWS

    def first_steps(send_a, keep_a, send_c, keep_c):
        got_a, got_c = swap(send_a, "tgt", 1), swap(send_c, "tgt", 2)
        send_a, keep_a = halve([keep_a], [got_a], 1)
        send_c, keep_c = halve([keep_c], [got_c], 0)
        got_a, got_c = swap(send_a, "tgt", 2), swap(send_c, "tgt", 1)
        bit = 2
        send, keep = halve([keep_a, keep_c], [got_a, got_c], bit)
        while send.shape[0] > 1:
            got = swap(send, "tgt", 1 << bit)
            bit += 1
            send, keep = halve([keep], [got], bit)
        return keep, swap(send, "tgt", 1 << bit)

    near = first_steps(*call(functools.partial(scores_near_kernel, tgt_size), outs, pool, right, flops=flops))
    far = first_steps(
        *call(
            functools.partial(scores_far_kernel, tgt_size, group, blocks, bs),
            outs, active, pool, mine, other, flops=flops, scratch=[pltpu.VMEM((k, 2 * PROWS), BF16)],
        )
    )
    out = ((part, 4 * PROWS), F32)
    return call(functools.partial(last_kernel, group), [out], *near, *far)[0]


def solution(mesh):
    return jax.shard_map(
        functools.partial(local, mesh.shape["tgt"], mesh.shape["pool"]),
        mesh=mesh,
        in_specs=(P("pool", "tgt"), P("pool", "tgt"), P("tgt", None, None), P()),
        out_specs=P(("pool", "tgt"), None),
        check_vma=False,
    )
```

```python
import functools

import jax
import jax.numpy as jnp
from jax import lax
from jax.experimental import pallas as pl
from jax.experimental.pallas import tpu as pltpu
from jax.sharding import PartitionSpec as P

PROWS = 128
F32, BF16 = jnp.float32, jnp.bfloat16
VMEM = pl.BlockSpec(memory_space=pltpu.VMEM)


def call(body, outs, *args, flops=0, mib=24, copies=0, far=(), kind=pltpu.VMEM):
    args = [pltpu.with_memory_space_constraint(x, pltpu.HBM) if n in far else x for n, x in enumerate(args)]
    specs = [pl.BlockSpec(memory_space=pltpu.HBM if n in far else pltpu.VMEM) for n in range(len(args))]
    return pl.pallas_call(
        body,
        in_specs=specs,
        out_specs=[VMEM] * len(outs),
        out_shape=[kind(shape, dtype) for shape, dtype in outs],
        scratch_shapes=[pltpu.SemaphoreType.DMA((copies,))] if copies else [],
        compiler_params=pltpu.CompilerParams(vmem_limit_bytes=mib * 2**20),
        cost_estimate=pl.CostEstimate(flops=flops, bytes_accessed=0, transcendentals=0),
    )(*args)


def copy_kernel(x, *rest):
    rest[-1][...] = x[...]


def after(x, *others, flops=0):
    return call(copy_kernel, [(x.shape, x.dtype)], x, *others, flops=flops)[0]


def place(group):
    return lax.axis_index("tgt"), lax.axis_index("pool") // group


def load(pairs, sems):
    copies = [pltpu.make_async_copy(src, dst, sems.at[n]) for n, (src, dst) in enumerate(pairs)]
    for copy in copies:
        copy.start()
    return copies


def order_of(parts, core):
    bits = list(range(parts.bit_length() - 1))
    return ([0, 1, 2] if core == 0 else [1, 0, 2]) + bits[3:]


def pick(core, values):
    return jnp.where(core == 1, values[1], values[0])


def row_block(parts, group, n):
    j, panel = place(group)
    away, away2, i = n < parts // 2, n % (parts // 2) < parts // 4, n % (parts // 4)
    at = []
    for core in range(2):
        first, second, *left = order_of(parts, core)
        value = (((j >> first) & 1) ^ away) << first | (((j >> second) & 1) ^ away2) << second
        for t, bit in enumerate(sorted(left)):
            value = value | ((i >> t) & 1) << bit
        at.append(value)
    return pick(panel & 1, at)


def rows_of(pool, parts, group, first, held):
    rows = pool.shape[0] // parts
    pairs = []
    for n in range(held.shape[0]):
        start = pl.multiple_of(row_block(parts, group, first + n) * rows, rows)
        pairs.append((pool.at[pl.ds(start, rows), :], held.at[n]))
    return pairs


def load_kernel(parts, group, blocks, pool, active, target, pre, table, target_v, pre_v, even, one, sems):
    copies = load([(active, table), (target, target_v), (pre, pre_v), *rows_of(pool, parts, group, 0, one)], sems)
    j, panel = place(group)
    base = panel - (panel & 1)
    copies[0].wait()
    shape = (even.shape[0], table.shape[1])
    n = lax.broadcasted_iota(jnp.int32, shape, 0)
    near, far = table[pl.ds(base, 1), :], table[pl.ds(base ^ 2, 1), :]
    listed = jnp.where(n < blocks, jnp.broadcast_to(near, shape), jnp.broadcast_to(far, shape))
    hits = (listed == j * blocks + n % blocks).astype(jnp.int32)
    even[...] = jnp.broadcast_to(jnp.max(hits, axis=1, keepdims=True), even.shape)
    for copy in copies[1:]:
        copy.wait()


def select_kernel(group, blocks, bs, evens, own, sib, rows, half):
    core = place(group)[1] & 1
    depth = blocks // 2
    for b in range(blocks):
        columns = slice(b * bs, (b + 1) * bs)
        value = jnp.where(evens[b : b + 1, :] != core, own[:, columns], sib[:, columns])
        rows[:, columns] = value

        @pl.when(core == b // depth)
        def _():
            half[:, (b % depth) * bs : (b % depth + 1) * bs] = value


def condition(scale, pre, even, rows_at, right):
    blocks, bs, _ = pre.shape
    for b in range(blocks):
        product = jnp.dot(rows_at(b), pre[b], preferred_element_type=F32)
        value = (product * scale).T.astype(BF16)
        listed, zero = even[b : b + 1, :PROWS] == 1, jnp.zeros_like(value)
        right[b * bs : (b + 1) * bs, :PROWS] = jnp.where(listed, value, zero)
        right[b * bs : (b + 1) * bs, PROWS:] = jnp.where(listed, zero, value)


def near_send_kernel(parts, group, scale, pool, evens, rows, pre, one, right, two, send, sems):
    copies = load(rows_of(pool, parts, group, parts // 4, two), sems)
    bs = pre.shape[1]
    condition(scale, pre, evens[: pre.shape[0], :], lambda b: rows[:, b * bs : (b + 1) * bs], right)
    scores([one], right, send)
    for copy in copies:
        copy.wait()


def far_send_kernel(group, scale, evens, mine, other, pre, one, *rest):
    right, send = rest[-2:]
    core = place(group)[1] & 1
    blocks, bs, _ = pre.shape
    depth = blocks // 2

    def rows_at(b):
        columns = slice((b % depth) * bs, (b % depth + 1) * bs)
        return jnp.where(core == b // depth, mine[:, columns], other[:, columns])

    condition(scale, pre, evens[blocks : 2 * blocks, :], rows_at, right)
    scores([one], right, send)


def scores(helds, right, *outs):
    for held, out in zip(helds, outs):
        for n in range(held.shape[0]):
            out[n] = jnp.dot(held[n], right[...], preferred_element_type=F32).astype(out.dtype)


def scores_kernel(held, right, *rest):
    scores([held], right, rest[-1])


def keep_kernel(three, four, right, *rest):
    scores([three, four], right, *rest[-2:])


def near_keep_kernel(parts, group, pool, right, _, keep, keep2, three, four, sems):
    copies = load(
        rows_of(pool, parts, group, parts // 2, three)
        + rows_of(pool, parts, group, parts // 2 + parts // 4, four), sems
    )
    for copy in copies:
        copy.wait()
    scores([three, four], right, keep, keep2)


def add_kernel(keep, got, *rest):
    rest[-1][...] = (keep[...] + got[...].astype(F32)).astype(BF16)


def halve_kernel(parts, group, step, gots, keep, *rest):
    send, home = rest[-2:]
    j, panel = place(group)
    bits = [sorted(order_of(parts, core)[2:])[step - 2] for core in range(2)]
    value = (j >> pick(panel & 1, bits)) & 1
    for i in range(send.shape[0]):
        for out, at in ((send, 2 * i + 1 - value), (home, 2 * i + value)):
            total = keep[at]
            for got in rest[:gots]:
                total = total + got[at].astype(F32)
            out[i] = total.astype(out.dtype)


def total_kernel(keep, got, *rest):
    rest[-1][...] = keep[0] + got[0].astype(F32)


def last_kernel(group, near, keep, got, out):
    pair = place(group)[1] >> 1
    width = near.shape[1]
    far = keep[0] + got[0].astype(F32)
    out[:, :width] = jnp.where(pair == 1, far, near[...])
    out[:, width:] = jnp.where(pair == 1, near[...], far)


def local(tgt_size, pool_size, pool, target, pre, active):
    blocks, bs, _ = pre.shape
    scale = (active.shape[1] * bs) ** (-0.5)
    group = PROWS // target.shape[0]
    m, k = pool.shape
    parts, part = tgt_size, m // tgt_size
    if group == 1:
        own = target
    else:
        groups = [list(range(g, g + group)) for g in range(0, pool_size, group)]
        own = lax.all_gather(target, "pool", axis=0, tiled=True, axis_index_groups=groups)

    def swap(x, axis, step):
        size = {"tgt": tgt_size, "pool": pool_size}[axis]
        return lax.ppermute(x, axis, [(i, i ^ step) for i in range(size)])

    sibling = swap(own, "pool", group)
    quarter = ((parts // 4, part, k), BF16)
    _, own_v, pre_v, evens, one = call(
        functools.partial(load_kernel, parts, group, blocks),
        [(active.shape, active.dtype), (own.shape, BF16), (pre.shape, BF16), ((2 * blocks, bs), active.dtype), quarter],
        pool, active, own, pre, copies=3 + parts // 4, far=(0, 1, 2, 3),
    )
    rows, half = call(
        functools.partial(select_kernel, group, blocks, bs), [((PROWS, k), BF16), ((PROWS, k // 2), BF16)],
        evens, own_v, sibling,
    )
    mine = swap(half, "pool", 2 * group)
    shape = (parts // 4, part, 2 * PROWS)
    right_out = ((k, 2 * PROWS), BF16)
    flops = 30 * m * k * PROWS

    def exchange(x, step):
        pairs = []
        for p in range(pool_size):
            bit = order_of(parts, (p // group) & 1)
            bit = bit[step] if step < 2 else sorted(bit[2:])[step - 2]
            pairs += [(p * parts + j, p * parts + (j ^ (1 << bit))) for j in range(parts)]
        return lax.ppermute(x, ("pool", "tgt"), pairs)

    def add(keep, got, *others):
        return call(add_kernel, [(shape, BF16)], keep, got, *others)[0]

    def rest(keep, gots, *others):
        step = 2
        while True:
            half_shape = (keep.shape[0] // 2,) + keep.shape[1:]
            send, keep = call(
                functools.partial(halve_kernel, parts, group, step, len(gots)),
                [(half_shape, BF16), (half_shape, F32)], keep, *gots, *others,
            )
            others, gots = (), [exchange(send, step)]
            step += 1
            if keep.shape[0] == 1:
                return keep, gots[0]

    right, two, send = call(
        functools.partial(near_send_kernel, parts, group, scale), [right_out, quarter, (shape, BF16)],
        pool, evens, rows, pre_v, one, flops=0, copies=parts // 4, far=(0,),
    )
    got = exchange(send, 0)
    send2 = call(scores_kernel, [(shape, BF16)], two, right, send)[0]
    got2 = exchange(send2, 0)
    keep, keep2, three, four = call(
        functools.partial(near_keep_kernel, parts, group), [(shape, F32)] * 2 + [quarter] * 2,
        pool, right, send2, flops=0, copies=parts // 2, far=(0,),
    )
    mine = after(mine, keep, flops=10**11)
    other = swap(mine, "pool", group)
    right, far_send = call(
        functools.partial(far_send_kernel, group, scale), [right_out, (shape, BF16)],
        evens, mine, other, pre_v, one, flops=0,
    )
    far_got = exchange(far_send, 0)
    far_send2 = call(scores_kernel, [(shape, BF16)], two, right, far_send)[0]
    far_got2 = exchange(far_send2, 0)
    got3 = exchange(add(keep, got), 1)
    far_keep, far_keep2 = call(keep_kernel, [(shape, F32)] * 2, three, four, right, flops=0)
    near = rest(keep2, [got2, got3], far_keep)
    near_total = call(total_kernel, [((part, 2 * PROWS), F32)], *near, far_got2, flops=10**11)[0]
    far_got3 = exchange(add(far_keep, far_got, near[0]), 1)
    far = rest(far_keep2, [far_got2, far_got3], near_total)
    out = ((part, 4 * PROWS), F32)
    return call(functools.partial(last_kernel, group), [out], near_total, *far, kind=jax.ShapeDtypeStruct)[0]


def solution(mesh):
    return jax.shard_map(
        functools.partial(local, mesh.shape["tgt"], mesh.shape["pool"]),
        mesh=mesh,
        in_specs=(P("pool", "tgt"), P("pool", "tgt"), P("tgt", None, None), P()),
        out_specs=P(("pool", "tgt"), None),
        check_vma=False,
    )
```

```python
import functools

import jax
import jax.numpy as jnp
from jax import lax
from jax.experimental import pallas as pl
from jax.experimental.pallas import tpu as pltpu
from jax.sharding import PartitionSpec as P

PROWS = 128
F32, BF16 = jnp.float32, jnp.bfloat16
VMEM = pl.BlockSpec(memory_space=pltpu.VMEM)


def call(body, outs, *args, flops=0, mib=24, copies=0, far=(), kind=pltpu.VMEM):
    args = [pltpu.with_memory_space_constraint(x, pltpu.HBM) if n in far else x for n, x in enumerate(args)]
    specs = [pl.BlockSpec(memory_space=pltpu.HBM if n in far else pltpu.VMEM) for n in range(len(args))]
    return pl.pallas_call(
        body,
        in_specs=specs,
        out_specs=[VMEM] * len(outs),
        out_shape=[kind(shape, dtype) for shape, dtype in outs],
        scratch_shapes=[pltpu.SemaphoreType.DMA((copies,))] if copies else [],
        compiler_params=pltpu.CompilerParams(vmem_limit_bytes=mib * 2**20),
        cost_estimate=pl.CostEstimate(flops=flops, bytes_accessed=0, transcendentals=0),
    )(*args)


def split_kernel(pieces, x, *rest):
    width = x.shape[1] // pieces
    for n, out in enumerate(rest[-pieces:]):
        out[...] = x[:, n * width : (n + 1) * width]


def split_after(x, pieces, *others, flops=0):
    outs = [((x.shape[0], x.shape[1] // pieces), x.dtype)] * pieces
    return call(functools.partial(split_kernel, pieces), outs, x, *others, flops=flops)


def place(group):
    return lax.axis_index("tgt"), lax.axis_index("pool") // group


def load(pairs, sems):
    copies = [pltpu.make_async_copy(src, dst, sems.at[n]) for n, (src, dst) in enumerate(pairs)]
    for copy in copies:
        copy.start()
    return copies


def order_of(parts, core):
    bits = list(range(parts.bit_length() - 1))
    return ([0, 1, 2] if core == 0 else [1, 0, 2]) + bits[3:]


def pick(core, values):
    return jnp.where(core == 1, values[1], values[0])


def row_block(parts, group, n):
    j, panel = place(group)
    away, away2, i = n < parts // 2, n % (parts // 2) < parts // 4, n % (parts // 4)
    at = []
    for core in range(2):
        first, second, *left = order_of(parts, core)
        value = (((j >> first) & 1) ^ away) << first | (((j >> second) & 1) ^ away2) << second
        for t, bit in enumerate(sorted(left)):
            value = value | ((i >> t) & 1) << bit
        at.append(value)
    return pick(panel & 1, at)


def load_kernel(group, blocks, active, target, pre, table, target_v, pre_v, even, sems):
    copies = load([(active, table), (target, target_v), (pre, pre_v)], sems)
    j, panel = place(group)
    base = panel - (panel & 1)
    copies[0].wait()
    shape = (even.shape[0], table.shape[1])
    n = lax.broadcasted_iota(jnp.int32, shape, 0)
    near, far = table[pl.ds(base, 1), :], table[pl.ds(base ^ 2, 1), :]
    listed = jnp.where(n < blocks, jnp.broadcast_to(near, shape), jnp.broadcast_to(far, shape))
    hits = (listed == j * blocks + n % blocks).astype(jnp.int32)
    even[...] = jnp.broadcast_to(jnp.max(hits, axis=1, keepdims=True), even.shape)
    for copy in copies[1:]:
        copy.wait()


def select_kernel(group, blocks, bs, evens, own, sib, rows, half):
    core = place(group)[1] & 1
    depth = blocks // 2
    for b in range(blocks):
        columns = slice(b * bs, (b + 1) * bs)
        value = jnp.where(evens[b : b + 1, :] != core, own[:, columns], sib[:, columns])
        rows[:, columns] = value

        @pl.when(core == b // depth)
        def _():
            half[:, (b % depth) * bs : (b % depth + 1) * bs] = value


def condition(scale, pre, even, rows_at, right):
    blocks, bs, _ = pre.shape
    for b in range(blocks):
        product = jnp.dot(rows_at(b), pre[b], preferred_element_type=F32)
        value = (product * scale).T.astype(BF16)
        listed, zero = even[b : b + 1, :PROWS] == 1, jnp.zeros_like(value)
        right[b * bs : (b + 1) * bs, :PROWS] = jnp.where(listed, value, zero)
        right[b * bs : (b + 1) * bs, PROWS:] = jnp.where(listed, zero, value)


def near_send_kernel(parts, group, scale, pool, evens, rows, pre, right, send):
    bs = pre.shape[1]
    condition(scale, pre, evens[: pre.shape[0], :], lambda b: rows[:, b * bs : (b + 1) * bs], right)
    scores(parts, group, 0, pool, right, send)


def far_send_kernel(parts, group, scale, pool, evens, pre, *rest):
    right, send = rest[-2:]
    core = place(group)[1] & 1
    blocks, bs, _ = pre.shape
    depth = blocks // 2

    def rows_at(b):
        return jnp.where(core == b // depth, rest[b % depth][...], rest[depth + b % depth][...])

    condition(scale, pre, evens[blocks : 2 * blocks, :], rows_at, right)
    scores(parts, group, 0, pool, right, send)


def scores(parts, group, quarter, pool, right, out):
    count, rows = out.shape[:2]
    for n in range(count):
        start = pl.multiple_of(row_block(parts, group, quarter * count + n) * rows, rows)
        value = jnp.dot(pool[pl.ds(start, rows), :], right[...], preferred_element_type=F32)
        out[n] = value.astype(out.dtype)


def scores_kernel(parts, group, quarters, pool, right, *rest):
    for quarter, out in zip(quarters, rest[-len(quarters) :]):
        scores(parts, group, quarter, pool, right, out)


def add_kernel(keep, got, *rest):
    rest[-1][...] = (keep[...] + got[...].astype(F32)).astype(BF16)


def halve_kernel(parts, group, step, gots, keep, *rest):
    send, home = rest[-2:]
    j, panel = place(group)
    bits = [sorted(order_of(parts, core)[2:])[step - 2] for core in range(2)]
    value = (j >> pick(panel & 1, bits)) & 1
    for i in range(send.shape[0]):
        for out, at in ((send, 2 * i + 1 - value), (home, 2 * i + value)):
            total = keep[at]
            for got in rest[:gots]:
                total = total + got[at].astype(F32)
            out[i] = total.astype(out.dtype)


def total_kernel(keep, got, *rest):
    rest[-1][...] = keep[0] + got[0].astype(F32)


def last_kernel(group, near, keep, got, out):
    pair = place(group)[1] >> 1
    width = near.shape[1]
    far = keep[0] + got[0].astype(F32)
    out[:, :width] = jnp.where(pair == 1, far, near[...])
    out[:, width:] = jnp.where(pair == 1, near[...], far)


def local(tgt_size, pool_size, pool, target, pre, active):
    blocks, bs, _ = pre.shape
    scale = (active.shape[1] * bs) ** (-0.5)
    group = PROWS // target.shape[0]
    m, k = pool.shape
    parts, part = tgt_size, m // tgt_size
    if group == 1:
        own = target
    else:
        groups = [list(range(g, g + group)) for g in range(0, pool_size, group)]
        own = lax.all_gather(target, "pool", axis=0, tiled=True, axis_index_groups=groups)

    def swap(x, axis, step):
        size = {"tgt": tgt_size, "pool": pool_size}[axis]
        return lax.ppermute(x, axis, [(i, i ^ step) for i in range(size)])

    sibling = swap(own, "pool", group)
    pool = pltpu.with_memory_space_constraint(pool, pltpu.VMEM)
    _, own_v, pre_v, evens = call(
        functools.partial(load_kernel, group, blocks),
        [(active.shape, active.dtype), (own.shape, BF16), (pre.shape, BF16), ((2 * blocks, bs), active.dtype)],
        active, own, pre, copies=3, far=(0, 1, 2), flops=5*10**9,
    )
    rows, half = call(
        functools.partial(select_kernel, group, blocks, bs), [((PROWS, k), BF16), ((PROWS, k // 2), BF16)],
        evens, own_v, sibling,
    )
    mine = swap(half, "pool", 2 * group)
    shape = (parts // 4, part, 2 * PROWS)
    right_out = ((k, 2 * PROWS), BF16)
    flops = 30 * m * k * PROWS

    def exchange(x, step):
        pairs = []
        for p in range(pool_size):
            bit = order_of(parts, (p // group) & 1)
            bit = bit[step] if step < 2 else sorted(bit[2:])[step - 2]
            pairs += [(p * parts + j, p * parts + (j ^ (1 << bit))) for j in range(parts)]
        return lax.ppermute(x, ("pool", "tgt"), pairs)

    def add(keep, got, *others):
        return call(add_kernel, [(shape, BF16)], keep, got, *others)[0]

    def rest(keep, gots, *others):
        step = 2
        while True:
            half_shape = (keep.shape[0] // 2,) + keep.shape[1:]
            send, keep = call(
                functools.partial(halve_kernel, parts, group, step, len(gots)),
                [(half_shape, BF16), (half_shape, F32)], keep, *gots, *others,
            )
            others, gots = (), [exchange(send, step)]
            step += 1
            if keep.shape[0] == 1:
                return keep, gots[0]

    right, send = call(
        functools.partial(near_send_kernel, parts, group, scale), [right_out, (shape, BF16)],
        pool, evens, rows, pre_v, flops=0,
    )
    got = exchange(send, 0)

    def more(quarters, dtype, right, *others, flops=0):
        body = functools.partial(scores_kernel, parts, group, quarters)
        return call(body, [(shape, dtype)] * len(quarters), pool, right, *others, flops=flops)

    send2 = more([1], BF16, right, send, flops=0)[0]
    got2 = exchange(send2, 0)
    keep, keep2 = more([2, 3], F32, right, send2, flops=0)
    mine = split_after(mine, blocks // 2, keep, flops=0)
    other = [swap(piece, "pool", group) for piece in mine]
    right, far_send = call(
        functools.partial(far_send_kernel, parts, group, scale), [right_out, (shape, BF16)],
        pool, evens, pre_v, *mine, *other, flops=0,
    )
    far_got = exchange(far_send, 0)
    far_send2 = more([1], BF16, right, far_send, got2)[0]
    far_got2 = exchange(far_send2, 0)
    got3 = exchange(add(keep, got), 1)
    far_keep, far_keep2 = more([2, 3], F32, right, flops=0)
    near = rest(keep2, [got2, got3], far_keep)
    near_total = call(total_kernel, [((part, 2 * PROWS), F32)], *near, far_got2, flops=10**11)[0]
    far_got3 = exchange(add(far_keep, far_got, near[0]), 1)
    far = rest(far_keep2, [far_got2, far_got3], near_total)
    out = ((part, 4 * PROWS), F32)
    return call(functools.partial(last_kernel, group), [out], near_total, *far, kind=jax.ShapeDtypeStruct)[0]


def solution(mesh):
    return jax.shard_map(
        functools.partial(local, mesh.shape["tgt"], mesh.shape["pool"]),
        mesh=mesh,
        in_specs=(P("pool", "tgt"), P("pool", "tgt"), P("tgt", None, None), P()),
        out_specs=P(("pool", "tgt"), None),
        check_vma=False,
    )
```

```python
import functools

import jax
import jax.numpy as jnp
from jax import lax
from jax.experimental import pallas as pl
from jax.experimental.pallas import tpu as pltpu
from jax.sharding import PartitionSpec as P

PROWS = 128
F32, BF16 = jnp.float32, jnp.bfloat16
VMEM = pl.BlockSpec(memory_space=pltpu.VMEM)


def call(body, outs, *args, flops=0, mib=24, copies=0, far=(), kind=pltpu.VMEM):
    args = [pltpu.with_memory_space_constraint(x, pltpu.HBM) if n in far else x for n, x in enumerate(args)]
    specs = [pl.BlockSpec(memory_space=pltpu.HBM if n in far else pltpu.VMEM) for n in range(len(args))]
    return pl.pallas_call(
        body,
        in_specs=specs,
        out_specs=[VMEM] * len(outs),
        out_shape=[kind(shape, dtype) for shape, dtype in outs],
        scratch_shapes=[pltpu.SemaphoreType.DMA((copies,))] if copies else [],
        compiler_params=pltpu.CompilerParams(vmem_limit_bytes=mib * 2**20),
        cost_estimate=pl.CostEstimate(flops=flops, bytes_accessed=0, transcendentals=0),
    )(*args)


def split_kernel(pieces, x, *rest):
    width = x.shape[1] // pieces
    for n, out in enumerate(rest[-pieces:]):
        out[...] = x[:, n * width : (n + 1) * width]


def split_after(x, pieces, *others, flops=0):
    outs = [((x.shape[0], x.shape[1] // pieces), x.dtype)] * pieces
    return call(functools.partial(split_kernel, pieces), outs, x, *others, flops=flops)


def place(group):
    return lax.axis_index("tgt"), lax.axis_index("pool") // group


def load(pairs, sems):
    copies = [pltpu.make_async_copy(src, dst, sems.at[n]) for n, (src, dst) in enumerate(pairs)]
    for copy in copies:
        copy.start()
    return copies


def order_of(parts, core):
    bits = list(range(parts.bit_length() - 1))
    return ([0, 1, 2] if core == 0 else [1, 0, 2]) + bits[3:]


def pick(core, values):
    return jnp.where(core == 1, values[1], values[0])


def row_block(parts, group, n):
    j, panel = place(group)
    away, away2, i = n < parts // 2, n % (parts // 2) < parts // 4, n % (parts // 4)
    at = []
    for core in range(2):
        first, second, *left = order_of(parts, core)
        value = (((j >> first) & 1) ^ away) << first | (((j >> second) & 1) ^ away2) << second
        for t, bit in enumerate(sorted(left)):
            value = value | ((i >> t) & 1) << bit
        at.append(value)
    return pick(panel & 1, at)


def load_kernel(group, blocks, active, target, table, target_v, even, sems):
    copies = load([(active, table), (target, target_v)], sems)
    j, panel = place(group)
    base = panel - (panel & 1)
    copies[0].wait()
    shape = (even.shape[0], table.shape[1])
    n = lax.broadcasted_iota(jnp.int32, shape, 0)
    near, far = table[pl.ds(base, 1), :], table[pl.ds(base ^ 2, 1), :]
    listed = jnp.where(n < blocks, jnp.broadcast_to(near, shape), jnp.broadcast_to(far, shape))
    hits = (listed == j * blocks + n % blocks).astype(jnp.int32)
    even[...] = jnp.broadcast_to(jnp.max(hits, axis=1, keepdims=True), even.shape)
    for copy in copies[1:]:
        copy.wait()


def select_kernel(group, blocks, bs, evens, own, sib, rows, half):
    core = place(group)[1] & 1
    depth = blocks // 2
    for b in range(blocks):
        columns = slice(b * bs, (b + 1) * bs)
        value = jnp.where(evens[b : b + 1, :] != core, own[:, columns], sib[:, columns])
        rows[:, columns] = value

        @pl.when(core == b // depth)
        def _():
            half[:, (b % depth) * bs : (b % depth + 1) * bs] = value


def condition(scale, pre, even, rows_at, right):
    blocks, bs, _ = pre.shape
    for b in range(blocks):
        product = jnp.dot(rows_at(b), pre[b], preferred_element_type=F32)
        value = (product * scale).T.astype(BF16)
        listed, zero = even[b : b + 1, :PROWS] == 1, jnp.zeros_like(value)
        right[b * bs : (b + 1) * bs, :PROWS] = jnp.where(listed, value, zero)
        right[b * bs : (b + 1) * bs, PROWS:] = jnp.where(listed, zero, value)


def near_send_kernel(parts, group, scale, pool, evens, rows, pre, right, send):
    bs = pre.shape[1]
    condition(scale, pre, evens[: pre.shape[0], :], lambda b: rows[:, b * bs : (b + 1) * bs], right)
    scores(parts, group, 0, pool, right, send)


def far_send_kernel(parts, group, scale, pool, evens, pre, *rest):
    right, send = rest[-2:]
    core = place(group)[1] & 1
    blocks, bs, _ = pre.shape
    depth = blocks // 2

    def rows_at(b):
        return jnp.where(core == b // depth, rest[b % depth][...], rest[depth + b % depth][...])

    condition(scale, pre, evens[blocks : 2 * blocks, :], rows_at, right)
    scores(parts, group, 0, pool, right, send)


def scores(parts, group, quarter, pool, right, out):
    count, rows = out.shape[:2]
    for n in range(count):
        start = pl.multiple_of(row_block(parts, group, quarter * count + n) * rows, rows)
        value = jnp.dot(pool[pl.ds(start, rows), :], right[...], preferred_element_type=F32)
        out[n] = value.astype(out.dtype)


def scores_kernel(parts, group, quarters, pool, right, *rest):
    for quarter, out in zip(quarters, rest[-len(quarters) :]):
        scores(parts, group, quarter, pool, right, out)


def add_kernel(keep, got, *rest):
    rest[-1][...] = (keep[...] + got[...].astype(F32)).astype(BF16)


def halve_kernel(parts, group, step, gots, keep, *rest):
    send, home = rest[-2:]
    j, panel = place(group)
    bits = [sorted(order_of(parts, core)[2:])[step - 2] for core in range(2)]
    value = (j >> pick(panel & 1, bits)) & 1
    for i in range(send.shape[0]):
        for out, at in ((send, 2 * i + 1 - value), (home, 2 * i + value)):
            total = keep[at]
            for got in rest[:gots]:
                total = total + got[at].astype(F32)
            out[i] = total.astype(out.dtype)


def total_kernel(keep, got, *rest):
    rest[-1][...] = keep[0] + got[0].astype(F32)


def last_kernel(group, near, keep, got, out):
    pair = place(group)[1] >> 1
    width = near.shape[1]
    far = keep[0] + got[0].astype(F32)
    out[:, :width] = jnp.where(pair == 1, far, near[...])
    out[:, width:] = jnp.where(pair == 1, near[...], far)


def local(tgt_size, pool_size, pool, target, pre, active):
    blocks, bs, _ = pre.shape
    scale = (active.shape[1] * bs) ** (-0.5)
    group = PROWS // target.shape[0]
    m, k = pool.shape
    parts, part = tgt_size, m // tgt_size
    if group == 1:
        own = target
    else:
        groups = [list(range(g, g + group)) for g in range(0, pool_size, group)]
        own = lax.all_gather(target, "pool", axis=0, tiled=True, axis_index_groups=groups)

    def swap(x, axis, step):
        size = {"tgt": tgt_size, "pool": pool_size}[axis]
        return lax.ppermute(x, axis, [(i, i ^ step) for i in range(size)])

    sibling = swap(own, "pool", group)
    pool = pltpu.with_memory_space_constraint(pool, pltpu.VMEM)
    pre = pltpu.with_memory_space_constraint(pre, pltpu.VMEM)
    _, own_v, evens = call(
        functools.partial(load_kernel, group, blocks),
        [(active.shape, active.dtype), (own.shape, BF16), ((2 * blocks, bs), active.dtype)],
        active, own, copies=2, far=(0, 1), flops=5*10**9,
    )
    rows, half = call(
        functools.partial(select_kernel, group, blocks, bs), [((PROWS, k), BF16), ((PROWS, k // 2), BF16)],
        evens, own_v, sibling,
    )
    mine = swap(half, "pool", 2 * group)
    shape = (parts // 4, part, 2 * PROWS)
    right_out = ((k, 2 * PROWS), BF16)
    flops = 30 * m * k * PROWS

    def exchange(x, step):
        pairs = []
        for p in range(pool_size):
            bit = order_of(parts, (p // group) & 1)
            bit = bit[step] if step < 2 else sorted(bit[2:])[step - 2]
            pairs += [(p * parts + j, p * parts + (j ^ (1 << bit))) for j in range(parts)]
        return lax.ppermute(x, ("pool", "tgt"), pairs)

    def add(keep, got, *others):
        return call(add_kernel, [(shape, BF16)], keep, got, *others)[0]

    def rest(keep, gots, *others):
        step = 2
        while True:
            half_shape = (keep.shape[0] // 2,) + keep.shape[1:]
            send, keep = call(
                functools.partial(halve_kernel, parts, group, step, len(gots)),
                [(half_shape, BF16), (half_shape, F32)], keep, *gots, *others,
            )
            others, gots = (), [exchange(send, step)]
            step += 1
            if keep.shape[0] == 1:
                return keep, gots[0]

    right, send = call(
        functools.partial(near_send_kernel, parts, group, scale), [right_out, (shape, BF16)],
        pool, evens, rows, pre, flops=0,
    )
    got = exchange(send, 0)

    def more(quarters, dtype, right, *others, flops=0):
        body = functools.partial(scores_kernel, parts, group, quarters)
        return call(body, [(shape, dtype)] * len(quarters), pool, right, *others, flops=flops)

    send2 = more([1], BF16, right, send, flops=0)[0]
    got2 = exchange(send2, 0)
    keep, keep2 = more([2, 3], F32, right, send2, flops=0)
    near_next = add(keep, got)
    mine = split_after(mine, blocks // 2, keep, flops=0)
    other = [swap(piece, "pool", group) for piece in mine]
    right, far_send = call(
        functools.partial(far_send_kernel, parts, group, scale), [right_out, (shape, BF16)],
        pool, evens, pre, *mine, *other, flops=0,
    )
    far_got = exchange(far_send, 0)
    far_send2 = more([1], BF16, right, far_send, got2)[0]
    far_got2 = exchange(far_send2, 0)
    got3 = exchange(near_next, 1)
    far_keep, far_keep2 = more([2, 3], F32, right, flops=0)
    near = rest(keep2, [got2, got3], far_keep)
    near_total = call(total_kernel, [((part, 2 * PROWS), F32)], *near, far_got2, flops=10**11)[0]
    far_next = add(far_keep, far_got, near[0])
    far_got3 = exchange(far_next, 1)
    far = rest(far_keep2, [far_got2, far_got3], near_total)
    out = ((part, 4 * PROWS), F32)
    return call(functools.partial(last_kernel, group), [out], near_total, *far, kind=jax.ShapeDtypeStruct)[0]


def solution(mesh):
    return jax.shard_map(
        functools.partial(local, mesh.shape["tgt"], mesh.shape["pool"]),
        mesh=mesh,
        in_specs=(P("pool", "tgt"), P("pool", "tgt"), P("tgt", None, None), P()),
        out_specs=P(("pool", "tgt"), None),
        check_vma=False,
    )
```

```python
import functools

import jax
import jax.numpy as jnp
from jax import lax
from jax.experimental import pallas as pl
from jax.experimental.pallas import tpu as pltpu
from jax.sharding import PartitionSpec as P

PROWS = 128
F32, BF16 = jnp.float32, jnp.bfloat16
VMEM = pl.BlockSpec(memory_space=pltpu.VMEM)


def call(body, outs, *args, flops=0, mib=24, copies=0, far=(), kind=pltpu.VMEM):
    args = [pltpu.with_memory_space_constraint(x, pltpu.HBM) if n in far else x for n, x in enumerate(args)]
    specs = [pl.BlockSpec(memory_space=pltpu.HBM if n in far else pltpu.VMEM) for n in range(len(args))]
    return pl.pallas_call(
        body,
        in_specs=specs,
        out_specs=[VMEM] * len(outs),
        out_shape=[kind(shape, dtype) for shape, dtype in outs],
        scratch_shapes=[pltpu.SemaphoreType.DMA((copies,))] if copies else [],
        compiler_params=pltpu.CompilerParams(vmem_limit_bytes=mib * 2**20),
        cost_estimate=pl.CostEstimate(flops=flops, bytes_accessed=0, transcendentals=0),
    )(*args)


def split_kernel(pieces, x, *rest):
    width = x.shape[1] // pieces
    for n, out in enumerate(rest[-pieces:]):
        out[...] = x[:, n * width : (n + 1) * width]


def split_after(x, pieces, *others, flops=0):
    outs = [((x.shape[0], x.shape[1] // pieces), x.dtype)] * pieces
    return call(functools.partial(split_kernel, pieces), outs, x, *others, flops=flops)


def place(group):
    return lax.axis_index("tgt"), lax.axis_index("pool") // group


def load(pairs, sems):
    copies = [pltpu.make_async_copy(src, dst, sems.at[n]) for n, (src, dst) in enumerate(pairs)]
    for copy in copies:
        copy.start()
    return copies


def order_of(parts, far, core):
    bits = list(range(parts.bit_length() - 1))
    return [[[0, 1, 2], [1, 0, 2]], [[0, 1, 2], [1, 0, 2]]][far][core] + bits[3:]


def pick(core, values):
    return jnp.where(core == 1, values[1], values[0])


def row_block(parts, group, far, n):
    j, panel = place(group)
    away, away2, i = n < parts // 2, n % (parts // 2) < parts // 4, n % (parts // 4)
    at = []
    for core in range(2):
        first, second, *left = order_of(parts, far, core)
        value = (((j >> first) & 1) ^ away) << first | (((j >> second) & 1) ^ away2) << second
        for t, bit in enumerate(sorted(left)):
            value = value | ((i >> t) & 1) << bit
        at.append(value)
    return pick(panel & 1, at)


def load_kernel(group, blocks, active, target, table, target_v, even, sems):
    copies = load([(active, table), (target, target_v)], sems)
    j, panel = place(group)
    base = panel - (panel & 1)
    copies[0].wait()
    shape = (even.shape[0], table.shape[1])
    n = lax.broadcasted_iota(jnp.int32, shape, 0)
    near, far = table[pl.ds(base, 1), :], table[pl.ds(base ^ 2, 1), :]
    listed = jnp.where(n < blocks, jnp.broadcast_to(near, shape), jnp.broadcast_to(far, shape))
    hits = (listed == j * blocks + n % blocks).astype(jnp.int32)
    even[...] = jnp.broadcast_to(jnp.max(hits, axis=1, keepdims=True), even.shape)
    for copy in copies[1:]:
        copy.wait()


def select_kernel(group, blocks, bs, evens, own, sib, rows, half):
    core = place(group)[1] & 1
    depth = blocks // 2
    for b in range(blocks):
        columns = slice(b * bs, (b + 1) * bs)
        value = jnp.where(evens[b : b + 1, :] != core, own[:, columns], sib[:, columns])
        rows[:, columns] = value

        @pl.when(core == b // depth)
        def _():
            half[:, (b % depth) * bs : (b % depth + 1) * bs] = value


def condition(scale, pre, even, rows_at, right):
    blocks, bs, _ = pre.shape
    for b in range(blocks):
        product = jnp.dot(rows_at(b), pre[b], preferred_element_type=F32)
        value = (product * scale).T.astype(BF16)
        listed, zero = even[b : b + 1, :PROWS] == 1, jnp.zeros_like(value)
        right[b * bs : (b + 1) * bs, :PROWS] = jnp.where(listed, value, zero)
        right[b * bs : (b + 1) * bs, PROWS:] = jnp.where(listed, zero, value)


def near_send_kernel(parts, group, scale, pool, evens, rows, pre, right, send):
    bs = pre.shape[1]
    condition(scale, pre, evens[: pre.shape[0], :], lambda b: rows[:, b * bs : (b + 1) * bs], right)
    scores(parts, group, 0, 0, pool, right, send)


def far_send_kernel(parts, group, scale, pool, evens, pre, *rest):
    right, send = rest[-2:]
    core = place(group)[1] & 1
    blocks, bs, _ = pre.shape
    depth = blocks // 2

    def rows_at(b):
        return jnp.where(core == b // depth, rest[b % depth][...], rest[depth + b % depth][...])

    condition(scale, pre, evens[blocks : 2 * blocks, :], rows_at, right)
    scores(parts, group, 1, 0, pool, right, send)


def scores(parts, group, far, quarter, pool, right, out):
    count, rows = out.shape[:2]
    for n in range(count):
        start = pl.multiple_of(row_block(parts, group, far, quarter * count + n) * rows, rows)
        value = jnp.dot(pool[pl.ds(start, rows), :], right[...], preferred_element_type=F32)
        out[n] = value.astype(out.dtype)


def scores_kernel(parts, group, far, quarters, pool, right, *rest):
    for quarter, out in zip(quarters, rest[-len(quarters) :]):
        scores(parts, group, far, quarter, pool, right, out)


def add_kernel(keep, got, *rest):
    rest[-1][...] = (keep[...] + got[...].astype(F32)).astype(BF16)


def add_two_kernel(keep, got, *rest):
    for n, out in enumerate(rest[-2:]):
        columns = slice(n * PROWS, (n + 1) * PROWS)
        out[...] = (keep[:, :, columns] + got[:, :, columns].astype(F32)).astype(BF16)


def halve_kernel(parts, group, far, step, gots, begin, keep, *rest):
    send, home = rest[-2:]
    j, panel = place(group)
    bits = [sorted(order_of(parts, far, core)[2:])[step - 2] for core in range(2)]
    value = (j >> pick(panel & 1, bits)) & 1
    for i in range(send.shape[0]):
        for out, at in ((send, 2 * i + 1 - value), (home, 2 * i + value)):
            width = out.shape[2]
            total = keep[at, :, begin : begin + width]
            for got in rest[:gots]:
                start = begin if got.shape[2] > width else 0
                total = total + got[at, :, start : start + width].astype(F32)
            out[i] = total.astype(out.dtype)


def total_kernel(keep, got, *rest):
    rest[-1][...] = keep[0] + got[0].astype(F32)


def last_kernel(group, near, keep, got, keep2, got2, out):
    pair = place(group)[1] >> 1
    width = near.shape[1]
    out[:, :width] = near[...]
    out[:, width:] = near[...]
    start = pl.multiple_of((1 - pair) * width, width)
    half = keep.shape[2]
    out[:, pl.ds(start, half)] = keep[0] + got[0].astype(F32)
    out[:, pl.ds(pl.multiple_of(start + half, half), half)] = keep2[0] + got2[0].astype(F32)


def local(tgt_size, pool_size, pool, target, pre, active):
    blocks, bs, _ = pre.shape
    scale = (active.shape[1] * bs) ** (-0.5)
    group = PROWS // target.shape[0]
    m, k = pool.shape
    parts, part = tgt_size, m // tgt_size
    if group == 1:
        own = target
    else:
        groups = [list(range(g, g + group)) for g in range(0, pool_size, group)]
        own = lax.all_gather(target, "pool", axis=0, tiled=True, axis_index_groups=groups)

    def swap(x, axis, step):
        size = {"tgt": tgt_size, "pool": pool_size}[axis]
        return lax.ppermute(x, axis, [(i, i ^ step) for i in range(size)])

    sibling = swap(own, "pool", group)
    pool = pltpu.with_memory_space_constraint(pool, pltpu.VMEM)
    pre = pltpu.with_memory_space_constraint(pre, pltpu.VMEM)
    _, own_v, evens = call(
        functools.partial(load_kernel, group, blocks),
        [(active.shape, active.dtype), (own.shape, BF16), ((2 * blocks, bs), active.dtype)],
        active, own, copies=2, far=(0, 1), flops=5*10**9,
    )
    rows, half = call(
        functools.partial(select_kernel, group, blocks, bs), [((PROWS, k), BF16), ((PROWS, k // 2), BF16)],
        evens, own_v, sibling,
    )
    mine = swap(half, "pool", 2 * group)
    shape = (parts // 4, part, 2 * PROWS)
    right_out = ((k, 2 * PROWS), BF16)
    flops = 30 * m * k * PROWS

    def exchange(x, step, far):
        pairs = []
        for p in range(pool_size):
            bit = order_of(parts, far, (p // group) & 1)
            bit = bit[step] if step < 2 else sorted(bit[2:])[step - 2]
            pairs += [(p * parts + j, p * parts + (j ^ (1 << bit))) for j in range(parts)]
        return lax.ppermute(x, ("pool", "tgt"), pairs)

    def add(keep, got, *others):
        return call(add_kernel, [(shape, BF16)], keep, got, *others)[0]

    def rest(far, keep, gots, *others, begin=0, width=2 * PROWS):
        step = 2
        while True:
            half_shape = (keep.shape[0] // 2, keep.shape[1], width)
            send, keep = call(
                functools.partial(halve_kernel, parts, group, far, step, len(gots), begin),
                [(half_shape, BF16), (half_shape, F32)], keep, *gots, *others,
            )
            others, gots, begin = (), [exchange(send, step, far)], 0
            step += 1
            if keep.shape[0] == 1:
                return keep, gots[0]

    right, send = call(
        functools.partial(near_send_kernel, parts, group, scale), [right_out, (shape, BF16)],
        pool, evens, rows, pre, flops=0,
    )
    got = exchange(send, 0, 0)

    def more(far, quarters, dtype, right, *others, flops=0):
        body = functools.partial(scores_kernel, parts, group, far, quarters)
        return call(body, [(shape, dtype)] * len(quarters), pool, right, *others, flops=flops)

    send2 = more(0, [1], BF16, right, send, flops=0)[0]
    got2 = exchange(send2, 0, 0)
    keep, keep2 = more(0, [2, 3], F32, right, send2, flops=0)
    near_next = add(keep, got)
    mine = split_after(mine, blocks // 2, keep, flops=0)
    other = [swap(piece, "pool", group) for piece in mine]
    right, far_send = call(
        functools.partial(far_send_kernel, parts, group, scale), [right_out, (shape, BF16)],
        pool, evens, pre, *mine, *other, flops=0,
    )
    far_got = exchange(far_send, 0, 1)
    far_send2 = more(1, [1], BF16, right, far_send, got2)[0]
    far_got2 = exchange(far_send2, 0, 1)
    got3 = exchange(near_next, 1, 0)
    far_keep, far_keep2 = more(1, [2, 3], F32, right, flops=0)
    near = rest(0, keep2, [got2, got3], far_keep)
    near_total = call(total_kernel, [((part, 2 * PROWS), F32)], *near, far_got2, flops=10**11)[0]
    far = []
    narrow = (shape[0], shape[1], PROWS)
    for begin, far_next in zip((0, PROWS), call(add_two_kernel, [(narrow, BF16)] * 2, far_keep, far_got, near[0])):
        gots = [far_got2, exchange(far_next, 1, 1)]
        far += rest(1, far_keep2, gots, near_total, begin=begin, width=PROWS)
    out = ((part, 4 * PROWS), F32)
    return call(functools.partial(last_kernel, group), [out], near_total, *far, kind=jax.ShapeDtypeStruct)[0]


def solution(mesh):
    return jax.shard_map(
        functools.partial(local, mesh.shape["tgt"], mesh.shape["pool"]),
        mesh=mesh,
        in_specs=(P("pool", "tgt"), P("pool", "tgt"), P("tgt", None, None), P()),
        out_specs=P(("pool", "tgt"), None),
        check_vma=False,
    )
```

```python
import functools

import jax
import jax.numpy as jnp
from jax import lax
from jax.experimental import pallas as pl
from jax.experimental.pallas import tpu as pltpu
from jax.sharding import PartitionSpec as P

PROWS = 128
F32, BF16 = jnp.float32, jnp.bfloat16
VMEM = pl.BlockSpec(memory_space=pltpu.VMEM)


def call(body, outs, *args, flops=0, mib=24, copies=0, far=(), kind=pltpu.VMEM):
    args = [pltpu.with_memory_space_constraint(x, pltpu.HBM) if n in far else x for n, x in enumerate(args)]
    specs = [pl.BlockSpec(memory_space=pltpu.HBM if n in far else pltpu.VMEM) for n in range(len(args))]
    return pl.pallas_call(
        body,
        in_specs=specs,
        out_specs=[VMEM] * len(outs),
        out_shape=[kind(shape, dtype) for shape, dtype in outs],
        scratch_shapes=[pltpu.SemaphoreType.DMA((copies,))] if copies else [],
        compiler_params=pltpu.CompilerParams(vmem_limit_bytes=mib * 2**20),
        cost_estimate=pl.CostEstimate(flops=flops, bytes_accessed=0, transcendentals=0),
    )(*args)


def split_kernel(pieces, x, *rest):
    width = x.shape[1] // pieces
    for n, out in enumerate(rest[-pieces:]):
        out[...] = x[:, n * width : (n + 1) * width]


def split_after(x, pieces, *others, flops=0):
    outs = [((x.shape[0], x.shape[1] // pieces), x.dtype)] * pieces
    return call(functools.partial(split_kernel, pieces), outs, x, *others, flops=flops)


def place(group):
    return lax.axis_index("tgt"), lax.axis_index("pool") // group


def load(pairs, sems):
    copies = [pltpu.make_async_copy(src, dst, sems.at[n]) for n, (src, dst) in enumerate(pairs)]
    for copy in copies:
        copy.start()
    return copies


def order_of(parts, far, core):
    bits = list(range(parts.bit_length() - 1))
    return [[[0, 1, 2], [1, 0, 2]], [[0, 1, 2], [1, 0, 2]]][far][core] + bits[3:]


def pick(core, values):
    return jnp.where(core == 1, values[1], values[0])


def row_block(parts, group, far, n):
    j, panel = place(group)
    away, away2, i = n < parts // 2, n % (parts // 2) < parts // 4, n % (parts // 4)
    at = []
    for core in range(2):
        first, second, *left = order_of(parts, far, core)
        value = (((j >> first) & 1) ^ away) << first | (((j >> second) & 1) ^ away2) << second
        for t, bit in enumerate(sorted(left)):
            value = value | ((i >> t) & 1) << bit
        at.append(value)
    return pick(panel & 1, at)


def load_kernel(group, blocks, active, target, table, target_v, even, sems):
    copies = load([(active, table), (target, target_v)], sems)
    j, panel = place(group)
    base = panel - (panel & 1)
    copies[0].wait()
    shape = (even.shape[0], table.shape[1])
    n = lax.broadcasted_iota(jnp.int32, shape, 0)
    near, far = table[pl.ds(base, 1), :], table[pl.ds(base ^ 2, 1), :]
    listed = jnp.where(n < blocks, jnp.broadcast_to(near, shape), jnp.broadcast_to(far, shape))
    hits = (listed == j * blocks + n % blocks).astype(jnp.int32)
    even[...] = jnp.broadcast_to(jnp.max(hits, axis=1, keepdims=True), even.shape)
    for copy in copies[1:]:
        copy.wait()


def select_kernel(group, blocks, bs, evens, own, sib, rows, half):
    core = place(group)[1] & 1
    depth = blocks // 2
    for b in range(blocks):
        columns = slice(b * bs, (b + 1) * bs)
        value = jnp.where(evens[b : b + 1, :] != core, own[:, columns], sib[:, columns])
        rows[:, columns] = value

        @pl.when(core == b // depth)
        def _():
            half[:, (b % depth) * bs : (b % depth + 1) * bs] = value


def condition(scale, pre, even, rows_at, right):
    blocks, bs, _ = pre.shape
    for b in range(blocks):
        product = jnp.dot(rows_at(b), pre[b], preferred_element_type=F32)
        value = (product * scale).T.astype(BF16)
        listed, zero = even[b : b + 1, :PROWS] == 1, jnp.zeros_like(value)
        right[b * bs : (b + 1) * bs, :PROWS] = jnp.where(listed, value, zero)
        right[b * bs : (b + 1) * bs, PROWS:] = jnp.where(listed, zero, value)


def near_send_kernel(parts, group, scale, pool, evens, rows, pre, right, send):
    bs = pre.shape[1]
    condition(scale, pre, evens[: pre.shape[0], :], lambda b: rows[:, b * bs : (b + 1) * bs], right)
    scores(parts, group, 0, 0, pool, right, send)


def far_send_kernel(parts, group, scale, pool, evens, pre, *rest):
    right, send = rest[-2:]
    core = place(group)[1] & 1
    blocks, bs, _ = pre.shape
    depth = blocks // 2

    def rows_at(b):
        return jnp.where(core == b // depth, rest[b % depth][...], rest[depth + b % depth][...])

    condition(scale, pre, evens[blocks : 2 * blocks, :], rows_at, right)
    scores(parts, group, 1, 0, pool, right, send)


def scores(parts, group, far, quarter, pool, right, out):
    count, rows = out.shape[:2]
    for n in range(count):
        start = pl.multiple_of(row_block(parts, group, far, quarter * count + n) * rows, rows)
        value = jnp.dot(pool[pl.ds(start, rows), :], right[...], preferred_element_type=F32)
        out[n] = value.astype(out.dtype)


def scores_kernel(parts, group, far, quarters, pool, right, *rest):
    for quarter, out in zip(quarters, rest[-len(quarters) :]):
        scores(parts, group, far, quarter, pool, right, out)


def add_kernel(keep, got, *rest):
    rest[-1][...] = (keep[...] + got[...].astype(F32)).astype(BF16)


def add_two_kernel(keep, got, *rest):
    for n, out in enumerate(rest[-2:]):
        columns = slice(n * PROWS, (n + 1) * PROWS)
        out[...] = (keep[:, :, columns] + got[:, :, columns].astype(F32)).astype(BF16)


def halve_kernel(parts, group, far, step, gots, begin, keep, *rest):
    send, home = rest[-2:]
    j, panel = place(group)
    bits = [sorted(order_of(parts, far, core)[2:])[step - 2] for core in range(2)]
    value = (j >> pick(panel & 1, bits)) & 1
    for i in range(send.shape[0]):
        for out, at in ((send, 2 * i + 1 - value), (home, 2 * i + value)):
            width = out.shape[2]
            total = keep[at, :, begin : begin + width]
            for got in rest[:gots]:
                start = begin if got.shape[2] > width else 0
                total = total + got[at, :, start : start + width].astype(F32)
            out[i] = total.astype(out.dtype)


def total_kernel(keep, got, *rest):
    rest[-1][...] = keep[0] + got[0].astype(F32)


def last_kernel(group, near, keep, got, keep2, got2, out):
    pair = place(group)[1] >> 1
    count, width, half = out.shape[0], near.shape[1], keep.shape[2]
    rows = pl.ds(pl.multiple_of(pl.program_id(0) * count, count), count)
    out[:, pl.ds(pl.multiple_of(pair * width, width), width)] = near[rows, :]
    start = pl.multiple_of((1 - pair) * width, width)
    out[:, pl.ds(start, half)] = keep[0, rows, :] + got[0, rows, :].astype(F32)
    start = pl.multiple_of(start + half, half)
    out[:, pl.ds(start, half)] = keep2[0, rows, :] + got2[0, rows, :].astype(F32)


def last(group, part, *args, steps=2):
    return pl.pallas_call(
        functools.partial(last_kernel, group),
        grid=(steps,),
        in_specs=[VMEM] * len(args),
        out_specs=pl.BlockSpec((part // steps, 4 * PROWS), lambda n: (n, 0)),
        out_shape=jax.ShapeDtypeStruct((part, 4 * PROWS), F32),
        compiler_params=pltpu.CompilerParams(vmem_limit_bytes=24 * 2**20),
        cost_estimate=pl.CostEstimate(flops=0, bytes_accessed=0, transcendentals=0),
    )(*args)


def local(tgt_size, pool_size, pool, target, pre, active):
    blocks, bs, _ = pre.shape
    scale = (active.shape[1] * bs) ** (-0.5)
    group = PROWS // target.shape[0]
    m, k = pool.shape
    parts, part = tgt_size, m // tgt_size
    if group == 1:
        own = target
    else:
        groups = [list(range(g, g + group)) for g in range(0, pool_size, group)]
        own = lax.all_gather(target, "pool", axis=0, tiled=True, axis_index_groups=groups)

    def swap(x, axis, step):
        size = {"tgt": tgt_size, "pool": pool_size}[axis]
        return lax.ppermute(x, axis, [(i, i ^ step) for i in range(size)])

    sibling = swap(own, "pool", group)
    pool = pltpu.with_memory_space_constraint(pool, pltpu.VMEM)
    pre = pltpu.with_memory_space_constraint(pre, pltpu.VMEM)
    _, own_v, evens = call(
        functools.partial(load_kernel, group, blocks),
        [(active.shape, active.dtype), (own.shape, BF16), ((2 * blocks, bs), active.dtype)],
        active, own, copies=2, far=(0, 1), flops=5*10**9,
    )
    rows, half = call(
        functools.partial(select_kernel, group, blocks, bs), [((PROWS, k), BF16), ((PROWS, k // 2), BF16)],
        evens, own_v, sibling,
    )
    mine = swap(half, "pool", 2 * group)
    shape = (parts // 4, part, 2 * PROWS)
    right_out = ((k, 2 * PROWS), BF16)
    flops = 30 * m * k * PROWS

    def exchange(x, step, far):
        pairs = []
        for p in range(pool_size):
            bit = order_of(parts, far, (p // group) & 1)
            bit = bit[step] if step < 2 else sorted(bit[2:])[step - 2]
            pairs += [(p * parts + j, p * parts + (j ^ (1 << bit))) for j in range(parts)]
        return lax.ppermute(x, ("pool", "tgt"), pairs)

    def add(keep, got, *others):
        return call(add_kernel, [(shape, BF16)], keep, got, *others)[0]

    def rest(far, keep, gots, *others, begin=0, width=2 * PROWS):
        step = 2
        while True:
            half_shape = (keep.shape[0] // 2, keep.shape[1], width)
            send, keep = call(
                functools.partial(halve_kernel, parts, group, far, step, len(gots), begin),
                [(half_shape, BF16), (half_shape, F32)], keep, *gots, *others,
            )
            others, gots, begin = (), [exchange(send, step, far)], 0
            step += 1
            if keep.shape[0] == 1:
                return keep, gots[0]

    right, send = call(
        functools.partial(near_send_kernel, parts, group, scale), [right_out, (shape, BF16)],
        pool, evens, rows, pre, flops=0,
    )
    got = exchange(send, 0, 0)

    def more(far, quarters, dtype, right, *others, flops=0):
        body = functools.partial(scores_kernel, parts, group, far, quarters)
        return call(body, [(shape, dtype)] * len(quarters), pool, right, *others, flops=flops)

    send2 = more(0, [1], BF16, right, send, flops=0)[0]
    got2 = exchange(send2, 0, 0)
    keep, keep2 = more(0, [2, 3], F32, right, send2, flops=0)
    near_next = add(keep, got)
    mine = split_after(mine, blocks // 2, keep, flops=0)
    other = [swap(piece, "pool", group) for piece in mine]
    right, far_send = call(
        functools.partial(far_send_kernel, parts, group, scale), [right_out, (shape, BF16)],
        pool, evens, pre, *mine, *other, flops=0,
    )
    far_got = exchange(far_send, 0, 1)
    far_send2 = more(1, [1], BF16, right, far_send, got2)[0]
    far_got2 = exchange(far_send2, 0, 1)
    got3 = exchange(near_next, 1, 0)
    far_keep, far_keep2 = more(1, [2, 3], F32, right, flops=0)
    near = rest(0, keep2, [got2, got3], far_keep)
    near_total = call(total_kernel, [((part, 2 * PROWS), F32)], *near, far_got2, flops=10**11)[0]
    far = []
    narrow = (shape[0], shape[1], PROWS)
    for begin, far_next in zip((0, PROWS), call(add_two_kernel, [(narrow, BF16)] * 2, far_keep, far_got, near[0])):
        gots = [far_got2, exchange(far_next, 1, 1)]
        far += rest(1, far_keep2, gots, near_total, begin=begin, width=PROWS)
    return last(group, part, near_total, *far)


def solution(mesh):
    return jax.shard_map(
        functools.partial(local, mesh.shape["tgt"], mesh.shape["pool"]),
        mesh=mesh,
        in_specs=(P("pool", "tgt"), P("pool", "tgt"), P("tgt", None, None), P()),
        out_specs=P(("pool", "tgt"), None),
        check_vma=False,
    )
```

```python
import functools

import jax
import jax.numpy as jnp
from jax import lax
from jax.experimental import pallas as pl
from jax.experimental.pallas import tpu as pltpu
from jax.sharding import PartitionSpec as P

PROWS = 128
F32, BF16 = jnp.float32, jnp.bfloat16
VMEM = pl.BlockSpec(memory_space=pltpu.VMEM)


def call(body, outs, *args, flops=0, mib=24, copies=0, far=(), kind=pltpu.VMEM):
    args = [pltpu.with_memory_space_constraint(x, pltpu.HBM) if n in far else x for n, x in enumerate(args)]
    specs = [pl.BlockSpec(memory_space=pltpu.HBM if n in far else pltpu.VMEM) for n in range(len(args))]
    return pl.pallas_call(
        body,
        in_specs=specs,
        out_specs=[VMEM] * len(outs),
        out_shape=[kind(shape, dtype) for shape, dtype in outs],
        scratch_shapes=[pltpu.SemaphoreType.DMA((copies,))] if copies else [],
        compiler_params=pltpu.CompilerParams(vmem_limit_bytes=mib * 2**20),
        cost_estimate=pl.CostEstimate(flops=flops, bytes_accessed=0, transcendentals=0),
    )(*args)


def split_kernel(pieces, x, *rest):
    width = x.shape[1] // pieces
    for n, out in enumerate(rest[-pieces:]):
        out[...] = x[:, n * width : (n + 1) * width]


def split_after(x, pieces, *others, flops=0):
    outs = [((x.shape[0], x.shape[1] // pieces), x.dtype)] * pieces
    return call(functools.partial(split_kernel, pieces), outs, x, *others, flops=flops)


def place(group):
    return lax.axis_index("tgt"), lax.axis_index("pool") // group


def load(pairs, sems):
    copies = [pltpu.make_async_copy(src, dst, sems.at[n]) for n, (src, dst) in enumerate(pairs)]
    for copy in copies:
        copy.start()
    return copies


def order_of(parts, far, core):
    bits = list(range(parts.bit_length() - 1))
    return [[[0, 1, 2], [1, 0, 2]], [[0, 1, 2], [1, 0, 2]]][far][core] + bits[3:]


def pick(core, values):
    return jnp.where(core == 1, values[1], values[0])


def row_block(parts, group, far, n):
    j, panel = place(group)
    away, away2, i = n < parts // 2, n % (parts // 2) < parts // 4, n % (parts // 4)
    at = []
    for core in range(2):
        first, second, *left = order_of(parts, far, core)
        value = (((j >> first) & 1) ^ away) << first | (((j >> second) & 1) ^ away2) << second
        for t, bit in enumerate(sorted(left)):
            value = value | ((i >> t) & 1) << bit
        at.append(value)
    return pick(panel & 1, at)


def load_kernel(group, blocks, active, target, table, target_v, even, sems):
    copies = load([(active, table), (target, target_v)], sems)
    j, panel = place(group)
    base = panel - (panel & 1)
    copies[0].wait()
    shape = (even.shape[0], table.shape[1])
    n = lax.broadcasted_iota(jnp.int32, shape, 0)
    near, far = table[pl.ds(base, 1), :], table[pl.ds(base ^ 2, 1), :]
    listed = jnp.where(n < blocks, jnp.broadcast_to(near, shape), jnp.broadcast_to(far, shape))
    hits = (listed == j * blocks + n % blocks).astype(jnp.int32)
    even[...] = jnp.broadcast_to(jnp.max(hits, axis=1, keepdims=True), even.shape)
    for copy in copies[1:]:
        copy.wait()


def select_kernel(group, blocks, bs, evens, own, sib, rows, half):
    core = place(group)[1] & 1
    depth = blocks // 2
    for b in range(blocks):
        columns = slice(b * bs, (b + 1) * bs)
        value = jnp.where(evens[b : b + 1, :] != core, own[:, columns], sib[:, columns])
        rows[:, columns] = value

        @pl.when(core == b // depth)
        def _():
            half[:, (b % depth) * bs : (b % depth + 1) * bs] = value


def condition(scale, pre, even, rows_at, right):
    blocks, bs, _ = pre.shape
    for b in range(blocks):
        product = jnp.dot(rows_at(b), pre[b], preferred_element_type=F32)
        value = (product * scale).T.astype(BF16)
        listed, zero = even[b : b + 1, :PROWS] == 1, jnp.zeros_like(value)
        right[b * bs : (b + 1) * bs, :PROWS] = jnp.where(listed, value, zero)
        right[b * bs : (b + 1) * bs, PROWS:] = jnp.where(listed, zero, value)


def near_send_kernel(parts, group, scale, pool, evens, rows, pre, right, send):
    bs = pre.shape[1]
    condition(scale, pre, evens[: pre.shape[0], :], lambda b: rows[:, b * bs : (b + 1) * bs], right)
    scores(parts, group, 0, 0, pool, right, send)


def far_send_kernel(parts, group, scale, pool, evens, pre, *rest):
    right, send = rest[-2:]
    core = place(group)[1] & 1
    blocks, bs, _ = pre.shape
    depth = blocks // 2

    def rows_at(b):
        return jnp.where(core == b // depth, rest[b % depth][...], rest[depth + b % depth][...])

    condition(scale, pre, evens[blocks : 2 * blocks, :], rows_at, right)
    scores(parts, group, 1, 0, pool, right, send)


def scores(parts, group, far, quarter, pool, right, out):
    count, rows = out.shape[:2]
    for n in range(count):
        start = pl.multiple_of(row_block(parts, group, far, quarter * count + n) * rows, rows)
        value = jnp.dot(pool[pl.ds(start, rows), :], right[...], preferred_element_type=F32)
        out[n] = value.astype(out.dtype)


def scores_kernel(parts, group, far, quarters, pool, right, *rest):
    for quarter, out in zip(quarters, rest[-len(quarters) :]):
        scores(parts, group, far, quarter, pool, right, out)


def add_kernel(keep, got, *rest):
    rest[-1][...] = (keep[...] + got[...].astype(F32)).astype(BF16)


def add_two_kernel(keep, got, *rest):
    for n, out in enumerate(rest[-2:]):
        columns = slice(n * PROWS, (n + 1) * PROWS)
        out[...] = (keep[:, :, columns] + got[:, :, columns].astype(F32)).astype(BF16)


def halve_kernel(parts, group, far, step, gots, begin, keep, *rest):
    send, home = rest[-2:]
    j, panel = place(group)
    bits = [sorted(order_of(parts, far, core)[2:])[step - 2] for core in range(2)]
    value = (j >> pick(panel & 1, bits)) & 1
    for i in range(send.shape[0]):
        for out, at in ((send, 2 * i + 1 - value), (home, 2 * i + value)):
            width = out.shape[2]
            total = keep[at, :, begin : begin + width]
            for got in rest[:gots]:
                start = begin if got.shape[2] > width else 0
                total = total + got[at, :, start : start + width].astype(F32)
            out[i] = total.astype(out.dtype)


def total_kernel(keep, got, keep2, got2, *rest):
    rest[-1][:, :PROWS] = keep[0] + got[0].astype(F32)
    rest[-1][:, PROWS:] = keep2[0] + got2[0].astype(F32)


def last_kernel(group, near, keep, got, keep2, got2, out):
    pair = place(group)[1] >> 1
    width = near.shape[1]
    out[:, :width] = near[...]
    out[:, width:] = near[...]
    start = pl.multiple_of((1 - pair) * width, width)
    half = keep.shape[2]
    out[:, pl.ds(start, half)] = keep[0] + got[0].astype(F32)
    out[:, pl.ds(pl.multiple_of(start + half, half), half)] = keep2[0] + got2[0].astype(F32)


def local(tgt_size, pool_size, pool, target, pre, active):
    blocks, bs, _ = pre.shape
    scale = (active.shape[1] * bs) ** (-0.5)
    group = PROWS // target.shape[0]
    m, k = pool.shape
    parts, part = tgt_size, m // tgt_size
    if group == 1:
        own = target
    else:
        groups = [list(range(g, g + group)) for g in range(0, pool_size, group)]
        own = lax.all_gather(target, "pool", axis=0, tiled=True, axis_index_groups=groups)

    def swap(x, axis, step):
        size = {"tgt": tgt_size, "pool": pool_size}[axis]
        return lax.ppermute(x, axis, [(i, i ^ step) for i in range(size)])

    sibling = swap(own, "pool", group)
    pool = pltpu.with_memory_space_constraint(pool, pltpu.VMEM)
    pre = pltpu.with_memory_space_constraint(pre, pltpu.VMEM)
    _, own_v, evens = call(
        functools.partial(load_kernel, group, blocks),
        [(active.shape, active.dtype), (own.shape, BF16), ((2 * blocks, bs), active.dtype)],
        active, own, copies=2, far=(0, 1), flops=5*10**9,
    )
    rows, half = call(
        functools.partial(select_kernel, group, blocks, bs), [((PROWS, k), BF16), ((PROWS, k // 2), BF16)],
        evens, own_v, sibling,
    )
    mine = swap(half, "pool", 2 * group)
    shape = (parts // 4, part, 2 * PROWS)
    right_out = ((k, 2 * PROWS), BF16)
    flops = 30 * m * k * PROWS

    def exchange(x, step, far):
        pairs = []
        for p in range(pool_size):
            bit = order_of(parts, far, (p // group) & 1)
            bit = bit[step] if step < 2 else sorted(bit[2:])[step - 2]
            pairs += [(p * parts + j, p * parts + (j ^ (1 << bit))) for j in range(parts)]
        return lax.ppermute(x, ("pool", "tgt"), pairs)

    def add(keep, got, *others):
        return call(add_kernel, [(shape, BF16)], keep, got, *others)[0]

    def rest(far, keep, gots, *others, begin=0, width=2 * PROWS):
        step = 2
        while True:
            half_shape = (keep.shape[0] // 2, keep.shape[1], width)
            send, keep = call(
                functools.partial(halve_kernel, parts, group, far, step, len(gots), begin),
                [(half_shape, BF16), (half_shape, F32)], keep, *gots, *others,
            )
            others, gots, begin = (), [exchange(send, step, far)], 0
            step += 1
            if keep.shape[0] == 1:
                return keep, gots[0]

    right, send = call(
        functools.partial(near_send_kernel, parts, group, scale), [right_out, (shape, BF16)],
        pool, evens, rows, pre, flops=0,
    )
    got = exchange(send, 0, 0)

    def more(far, quarters, dtype, right, *others, flops=0):
        body = functools.partial(scores_kernel, parts, group, far, quarters)
        return call(body, [(shape, dtype)] * len(quarters), pool, right, *others, flops=flops)

    send2 = more(0, [1], BF16, right, send, flops=0)[0]
    got2 = exchange(send2, 0, 0)
    keep, keep2 = more(0, [2, 3], F32, right, send2, flops=0)
    narrow = (shape[0], shape[1], PROWS)
    near_next = call(add_two_kernel, [(narrow, BF16)] * 2, keep, got)
    mine = split_after(mine, blocks // 2, keep, flops=0)
    other = [swap(piece, "pool", group) for piece in mine]
    right, far_send = call(
        functools.partial(far_send_kernel, parts, group, scale), [right_out, (shape, BF16)],
        pool, evens, pre, *mine, *other, flops=0,
    )
    far_got = exchange(far_send, 0, 1)
    far_send2 = more(1, [1], BF16, right, far_send, got2)[0]
    far_got2 = exchange(far_send2, 0, 1)
    got3 = [exchange(piece, 1, 0) for piece in near_next]
    far_keep, far_keep2 = more(1, [2, 3], F32, right, flops=10**10)
    near = []
    for n, piece in enumerate(got3):
        near += rest(0, keep2, [got2, piece], far_keep, begin=n * PROWS, width=PROWS)
    near_total = call(total_kernel, [((part, 2 * PROWS), F32)], *near, far_got2, flops=10**11)[0]
    far = []
    narrow = (shape[0], shape[1], PROWS)
    for begin, far_next in zip((0, PROWS), call(add_two_kernel, [(narrow, BF16)] * 2, far_keep, far_got, near[0], near[2])):
        gots = [far_got2, exchange(far_next, 1, 1)]
        far += rest(1, far_keep2, gots, near_total, begin=begin, width=PROWS)
    out = ((part, 4 * PROWS), F32)
    return call(functools.partial(last_kernel, group), [out], near_total, *far, kind=jax.ShapeDtypeStruct)[0]


def solution(mesh):
    return jax.shard_map(
        functools.partial(local, mesh.shape["tgt"], mesh.shape["pool"]),
        mesh=mesh,
        in_specs=(P("pool", "tgt"), P("pool", "tgt"), P("tgt", None, None), P()),
        out_specs=P(("pool", "tgt"), None),
        check_vma=False,
    )
```
